256 devices in a mesh: rows: 256 (over x, z, y, core).
Axes of the slice: x: 4, y: 4, z: 8, core: 2. Of those that a mesh axis runs over, the one named last changes fastest.
Arguments:
- vectors: bfloat16 [8, 2097152], P(None, 'rows'), may hold values from -6 to 6
- basis_leaf: bfloat16 [32, 2097152], P(None, 'rows'), may hold values from -0.75 to 0.75
- near_block: bfloat16 [6, 64, 2097152], P(None, None, 'rows'), may hold values from -0.3125 to 0.3125
- near_index: int32 [6, 32768], P(None, 'rows'), may hold values from 0 to 32767, as said below
- near_count: int32 [32768], P('rows'), may hold values from 1 to 6
- leaf_trans: bfloat16 [32, 32, 32768], P(None, None, 'rows'), may hold values from -0.5 to 0.5
- leaf_coupling: bfloat16 [8, 32, 32, 32768], P(None, None, None, 'rows'), may hold values from -0.375 to 0.375
- leaf_index: int32 [8, 32768], P(None, 'rows'), may hold values from 0 to 32767, as said below
- cluster_trans: bfloat16 [32, 32, 4096], P(None, None, 'rows'), may hold values from -0.5 to 0.5
- cluster_coupling: bfloat16 [3, 32, 32, 4096], P(None, None, None, 'rows'), may hold values from -0.625 to 0.625
- cluster_index: int32 [3, 4096], P(None, 'rows'), may hold values from 0 to 4095, as said below
- cluster_count: int32 [4096], P('rows'), may hold values from 1 to 3, as said below
- middle_trans: bfloat16 [32, 32, 512], P(None, None, 'rows'), may hold values from -0.5 to 0.5
- middle_coupling: bfloat16 [8, 32, 32, 512], P(None, None, None, 'rows'), may hold values from -0.375 to 0.375
- middle_index: int32 [8, 512], P(None, 'rows'), may hold values from 0 to 511, as said below
- middle_count: int32 [512], P('rows'), may hold values from 1 to 8
- top_coupling: bfloat16 [8, 32, 32, 64], replicated, may hold values from -0.375 to 0.375
- top_index: int32 [8, 64], replicated, may hold values from 0 to 63, as said below
Outputs:
- product: bfloat16 [8, 2097152], P(None, 'rows')
The draws below stay inside these ranges and needn't reach their ends.
Inputs may be any that keep to these rules, and one draw needn't show every extreme that they name: near_index[s, i] is a leaf within 4 leaves of leaf i; slot 0 is i itself; the first near_count[i] slots are distinct. leaf_index[s, i] lies in the second-level clusters k - 2 to k + 2, k the cluster of leaf i, and more than 4 leaves from i; distinct over s. cluster_index[s, k] is a cluster within 2 clusters of k, not k; the first slots hold k + 1 and then k - 1, those of them that exist; the first cluster_count[k] slots are distinct. cluster_count[k] is 2 or more wherever k has two or more partners within reach, except for cluster 0. middle_index[s, j] is any cluster of that level but j; the first middle_count[j] slots are distinct. top_index[s, g] are distinct top clusters other than g.
All inputs are finite; a program needn't handle non-finite values.
Results may differ from the reference program's by a relative error of at most 0.01.
Values may be sent and summed in bfloat16 or wider, within the bound.
No kernel may reach another device: no remote copies, remote signals or barrier semaphores. Data moves between devices by JAX's collectives and lax.ppermute only.
A program may use at most 128 MiB of HBM per device.

```python
import jax
import jax.numpy as jnp
from jax import lax

LEAF = 64
RANK = 32
NV = 8
BRANCH = 8
NEAR = 6
NEARW = 4
FARW = 2
LEAF_COUP = 8
CLUSTER_COUP = 3
MIDDLE_COUP = 8
LEAVES = 32768
POINTS = 2097152
CLUSTERS = 4096
MIDDLES = 512
TOPS = 64
TOP_COUP = 8


def pick_window(key, item_count, slot_count, group_size, reach_span, inner_gap, keep_self, adjacent_first):
    positions = jnp.arange(item_count, dtype=jnp.int32)[:, None]
    span_size = (2 * reach_span + 1) * group_size
    offsets = jnp.arange(span_size, dtype=jnp.int32)[None, :]
    candidate = positions // group_size * group_size - reach_span * group_size + offsets
    usable = (candidate >= 0) & (candidate < item_count) & (jnp.abs(candidate - positions) > inner_gap)
    scores = jax.random.randint(key, (item_count, span_size), 0, 1 << 16) * span_size + offsets
    scores = jnp.where(usable, scores, -1 - offsets)
    top_score = (1 << 16) * span_size + span_size
    if keep_self:
        scores = jnp.where(candidate == positions, top_score, scores)
    if adjacent_first:
        scores = jnp.where(usable & (candidate == positions + 1), top_score + 2, scores)
        scores = jnp.where(usable & (candidate == positions - 1), top_score + 1, scores)
    ranked = lax.top_k(scores, slot_count)[1]
    picked = jnp.take_along_axis(candidate, ranked, axis=1)
    usable_count = usable.sum(axis=1).astype(jnp.int32)
    rank_ok = jnp.arange(slot_count, dtype=jnp.int32)[None, :] < usable_count[:, None]
    picked = jnp.where(rank_ok, picked, positions)
    return (picked.T.astype(jnp.int32), usable_count)


def pick_count(key, usable_count, slot_count, least):
    item_count = usable_count.shape[0]
    raw_count = jax.random.randint(key, (item_count,), least, slot_count + 1)
    counts = jnp.minimum(raw_count, usable_count)
    counts = counts.at[item_count // 2].set(jnp.minimum(slot_count, usable_count[item_count // 2]))
    counts = counts.at[0].set(1)
    return counts.astype(jnp.int32)


def draw_near_index(key, part):
    return pick_window(jax.random.fold_in(key, 101), LEAVES, NEAR, 1, NEARW, -1, True, False)[0]


def draw_near_count(key, part):
    usable_count = pick_window(jax.random.fold_in(key, 101), LEAVES, NEAR, 1, NEARW, -1, True, False)[1]
    key = jax.random.fold_in(key, 1)
    return pick_count(key, usable_count, NEAR, 1)


def draw_leaf_index(key, part):
    key = jax.random.fold_in(key, 2)
    return pick_window(key, LEAVES, LEAF_COUP, BRANCH, FARW, NEARW, False, False)[0]


def draw_cluster_index(key, part):
    return pick_window(jax.random.fold_in(key, 103), CLUSTERS, CLUSTER_COUP, 1, FARW, 0, False, True)[0]


def draw_cluster_count(key, part):
    usable_count = pick_window(jax.random.fold_in(key, 103), CLUSTERS, CLUSTER_COUP, 1, FARW, 0, False, True)[1]
    key = jax.random.fold_in(key, 3)
    return pick_count(key, usable_count, CLUSTER_COUP, 2)


def draw_middle_index(key, part):
    return pick_window(jax.random.fold_in(key, 104), MIDDLES, MIDDLE_COUP, 1, MIDDLES, 0, False, False)[0]


def draw_middle_count(key, part):
    usable_count = pick_window(jax.random.fold_in(key, 104), MIDDLES, MIDDLE_COUP, 1, MIDDLES, 0, False, False)[1]
    key = jax.random.fold_in(key, 4)
    return pick_count(key, usable_count, MIDDLE_COUP, 1)


def draw_top_index(key, part):
    key = jax.random.fold_in(key, 5)
    return pick_window(key, TOPS, TOP_COUP, 1, TOPS, 0, False, False)[0]


def steps_of(stream_key, extent, cuts, low, largest):
    def one(axis_at, shards_of):
        steps = jax.random.uniform(jax.random.fold_in(jax.random.fold_in(stream_key, 6), axis_at), (shards_of,), jnp.float32, low / len(cuts), largest / len(cuts))
        return jnp.repeat(jnp.exp(steps), extent[axis_at] // shards_of).reshape((-1,) + (1,) * (len(extent) - axis_at - 1))

    level = one(*cuts[0])
    for cut in cuts[1:]:
        level = level * one(*cut)
    return level


def centred(stream_key, shape, deviation, reach, cuts=(), kind=jnp.bfloat16):
    factor_of = steps_of(stream_key, shape, cuts, -0.22, 0.18) if cuts else 1.0
    entries = jax.random.normal(stream_key, shape, jnp.float32) * deviation * factor_of
    return jnp.minimum(jnp.maximum(entries, -reach), reach).astype(kind)


def setup_inputs(seed: int = 0) -> dict:
    key_of = jax.random.split(jax.random.key(seed), 19)
    return {
        "vectors": centred(key_of[0], (NV, POINTS), 1.0, 6.0, ((1, 256),)),
        "basis_leaf": centred(key_of[1], (RANK, POINTS), LEAF ** -0.5, 0.75, ((1, 256),)),
        "near_block": centred(key_of[2], (NEAR, LEAF, POINTS), (NEAR * LEAF) ** -0.5, 0.3125, ((2, 256),)),
        "near_index": draw_near_index(jax.random.fold_in(key_of[18], 71), 0),
        "near_count": draw_near_count(jax.random.fold_in(key_of[18], 71), 0),
        "leaf_trans": centred(key_of[5], (RANK, RANK, LEAVES), (4 * RANK) ** -0.5, 0.5, ((2, 256),)),
        "leaf_coupling": centred(key_of[6], (LEAF_COUP, RANK, RANK, LEAVES), (LEAF_COUP * RANK) ** -0.5, 0.375, ((3, 256),)),
        "leaf_index": draw_leaf_index(jax.random.fold_in(key_of[18], 71), 0),
        "cluster_trans": centred(key_of[8], (RANK, RANK, CLUSTERS), (4 * RANK) ** -0.5, 0.5, ((2, 256),)),
        "cluster_coupling": centred(key_of[9], (CLUSTER_COUP, RANK, RANK, CLUSTERS), (CLUSTER_COUP * RANK) ** -0.5, 0.625, ((3, 256),)),
        "cluster_index": draw_cluster_index(jax.random.fold_in(key_of[18], 71), 0),
        "cluster_count": draw_cluster_count(jax.random.fold_in(key_of[18], 71), 0),
        "middle_trans": centred(key_of[12], (RANK, RANK, MIDDLES), (4 * RANK) ** -0.5, 0.5, ((2, 256),)),
        "middle_coupling": centred(key_of[13], (MIDDLE_COUP, RANK, RANK, MIDDLES), (MIDDLE_COUP * RANK) ** -0.5, 0.375, ((3, 256),)),
        "middle_index": draw_middle_index(jax.random.fold_in(key_of[18], 71), 0),
        "middle_count": draw_middle_count(jax.random.fold_in(key_of[18], 71), 0),
        "top_coupling": centred(key_of[16], (TOP_COUP, RANK, RANK, TOPS), (TOP_COUP * RANK) ** -0.5, 0.375),
        "top_index": draw_top_index(jax.random.fold_in(key_of[18], 71), 0),
    }


def upward(children, transfer):
    products = jnp.einsum('vrn,rqn->vqn', children.astype(jnp.float32), transfer.astype(jnp.float32))
    return products.reshape(products.shape[0], products.shape[1], -1, BRANCH).sum(axis=3)


def couple(coefs, coupling, index, counts):
    def one_slot(running, packed):
        column, weights, slot_id = packed
        picked = jnp.take(coefs, column, axis=2).astype(jnp.float32)
        usable = (slot_id < counts).astype(jnp.float32)
        contrib = jnp.einsum('vrn,rqn->vqn', picked, weights.astype(jnp.float32))
        return running + contrib * usable[None, None, :], None
    initial = jnp.zeros((coefs.shape[0], coupling.shape[2], coefs.shape[2]), jnp.float32)
    slot_ids = jnp.arange(index.shape[0], dtype=jnp.int32)
    return lax.scan(one_slot, initial, (index, coupling, slot_ids))[0]


def reference(vectors, basis_leaf, near_block, near_index, near_count, leaf_trans, leaf_coupling, leaf_index, cluster_trans, cluster_coupling, cluster_index, cluster_count, middle_trans, middle_coupling, middle_index, middle_count, top_coupling, top_index):
    leaves_all = vectors.reshape(NV, LEAVES, LEAF)
    basis_all = basis_leaf.reshape(RANK, LEAVES, LEAF)
    leaf_coef = jnp.einsum('via,ria->vri', leaves_all.astype(jnp.float32), basis_all.astype(jnp.float32)).astype(jnp.bfloat16)
    cluster_coef = upward(leaf_coef, leaf_trans).astype(jnp.bfloat16)
    middle_coef = upward(cluster_coef, cluster_trans).astype(jnp.bfloat16)
    top_coef = upward(middle_coef, middle_trans).astype(jnp.bfloat16)
    picked_top = jnp.take(top_coef, top_index, axis=2).astype(jnp.float32)
    top_field = jnp.einsum('vrsg,srqg->vqg', picked_top, top_coupling.astype(jnp.float32)).astype(jnp.bfloat16)
    middle_near = couple(middle_coef, middle_coupling, middle_index, middle_count)
    middle_down = jnp.einsum('vqj,rqj->vrj', jnp.repeat(top_field, BRANCH, axis=2).astype(jnp.float32), middle_trans.astype(jnp.float32))
    middle_field = (middle_near + middle_down).astype(jnp.bfloat16)
    cluster_near = couple(cluster_coef, cluster_coupling, cluster_index, cluster_count)
    cluster_down = jnp.einsum('vqk,rqk->vrk', jnp.repeat(middle_field, BRANCH, axis=2).astype(jnp.float32), cluster_trans.astype(jnp.float32))
    cluster_field = (cluster_near + cluster_down).astype(jnp.bfloat16)
    full_counts = jnp.full((LEAVES,), LEAF_COUP, jnp.int32)
    leaf_near = couple(leaf_coef, leaf_coupling, leaf_index, full_counts)
    leaf_down = jnp.einsum('vqi,rqi->vri', jnp.repeat(cluster_field, BRANCH, axis=2).astype(jnp.float32), leaf_trans.astype(jnp.float32))
    leaf_field = (leaf_near + leaf_down).astype(jnp.bfloat16)
    blocks = near_block.reshape(NEAR, LEAF, LEAVES, LEAF)

    def near_slot(running, packed):
        column, block, slot_id = packed
        picked = jnp.take(leaves_all, column, axis=1).astype(jnp.float32)
        usable = (slot_id < near_count).astype(jnp.float32)
        contrib = jnp.einsum('vib,bia->via', picked * usable[None, :, None], block.astype(jnp.float32))
        return running + contrib, None

    initial = jnp.zeros((NV, LEAVES, LEAF), jnp.float32)
    slot_ids = jnp.arange(NEAR, dtype=jnp.int32)
    near_part = lax.scan(near_slot, initial, (near_index, blocks, slot_ids))[0]
    far_part = jnp.einsum('vri,ria->via', leaf_field.astype(jnp.float32), basis_all.astype(jnp.float32))
    return (near_part + far_part).reshape(NV, POINTS).astype(jnp.bfloat16)
```

```python
import jax
import jax.numpy as jnp
from jax import lax
from jax.experimental import pallas as pl
from jax.experimental.pallas import tpu as pltpu
from jax.sharding import PartitionSpec as P

F32 = jnp.float32
BF = jnp.bfloat16
I32 = jnp.int32
NT = (((1,), (1,)), ((), ()))
MIB = 1 << 20


def iota(shape, dim):
    return lax.broadcasted_iota(I32, shape, dim)


def mm(a, b):
    return jnp.dot(a, b, preferred_element_type=F32)


def mm_nt(a, b):
    return lax.dot_general(a, b, NT, preferred_element_type=F32)


def halves(x):
    hi = x.astype(BF)
    return hi, (x - hi.astype(F32)).astype(BF)


def fetch(sems, *pairs):
    copies = [pltpu.make_async_copy(a, b, sems.at[n]) for n, (a, b) in enumerate(pairs)]
    for c in copies:
        c.start()
    return copies


def upward_kernel(
    vec_h, basis_h, lt_h, ct_h, mt_h,
    payload, near_msg, far_msg, lc, cl, basis, lt, ct, mt,
    vec, rows, lcs, sems,
):
    copies = fetch(sems, (vec_h, vec), (basis_h, basis), (mt_h, mt), (lt_h, lt), (ct_h, ct))
    even = lax.axis_index("rows") % 2 == 0
    own = (iota((32, 256), 1) // 64 == iota((32, 256), 0) // 8).astype(F32)
    eye = (iota((32, 32), 0) == iota((32, 32), 1)).astype(BF)
    for copy in copies[:3]:
        copy.wait()
    mtf = mt[...].astype(F32)
    mtj = [mtf[:, j, :].astype(BF) for j in range(2)]
    for c in range(32):
        x = vec[:, c * 256 : (c + 1) * 256].astype(F32)
        x = (jnp.concatenate([x] * 4, axis=0) * own).astype(BF)
        rows[c * 32 : (c + 1) * 32, 0:32] = mm_nt(x, basis[:, c * 256 : (c + 1) * 256])
    group = iota((32, 128), 1) // 16
    first = jnp.zeros((32, 128), F32)
    last = jnp.zeros((32, 128), F32)
    for v in range(8):
        x = rows[pl.ds(v, 128, stride=8), :][:, 0:32].astype(BF)
        x = mm_nt(eye, x)
        lcs[:, v * 128 : (v + 1) * 128] = x
        first = jnp.where(group == v, pltpu.roll(x, v * 16, 1) if v else x, first)
        last = jnp.where(group == v, pltpu.roll(x, v * 16 + 16, 1) if v < 7 else x, last)
    lc[...] = lcs[...].astype(BF)
    copies[3].wait()
    sums = [jnp.zeros((32, 128), F32) for _ in range(8)]
    for r in range(32):
        w = lt[r].astype(F32)
        for v in range(8):
            sums[v] = sums[v] + w * lcs[r : r + 1, v * 128 : (v + 1) * 128]
    hi, lo = halves(jnp.concatenate(sums, axis=0))
    spread = (iota((128, 128), 0) // 8 == iota((128, 128), 1) % 16).astype(BF)
    y = mm(hi, spread) + mm(lo, spread)
    c = jnp.zeros((32, 128), F32)
    for v in range(8):
        c = jnp.where(group == v, y[v * 32 : (v + 1) * 32], c)
    y = jnp.concatenate([y] * 4, axis=1)
    y = jnp.where(iota((256, 512), 0) % 32 == iota((256, 512), 1) // 16, y, 0.0).astype(BF)
    gather = (iota((8, 256), 0) == iota((8, 256), 1) // 32).astype(BF)
    y = mm(gather, y)
    half = iota((8, 512), 1) % 16 // 8
    copies[4].wait()
    pieces = []
    top = jnp.zeros((8, 32), F32)
    for j in range(2):
        m = mm(jnp.where(half == j, y, 0.0).astype(BF), ct[...]).astype(BF)
        pieces.append(m.astype(F32))
        top = top + mm(m, mtj[j])
    hi = top.astype(BF).astype(F32)
    out = jnp.concatenate(pieces + [hi, top - hi], axis=1).astype(BF)
    for z in range(8):
        payload[z] = out
    c = c.astype(BF)
    cl[...] = c
    head = vec[:, 0:256].astype(F32)
    tail = vec[:, 8192 - 256 : 8192].astype(F32)
    for ref, right in ((near_msg, even), (far_msg, jnp.logical_not(even))):
        ref[0:32, :] = jnp.where(right, last, first).astype(BF)
        ref[32:64, :] = c
        pts = jnp.where(right, tail, head)
        ref[64:80, :] = jnp.concatenate([pts[:, 0:128], pts[:, 128:256]], axis=0).astype(BF)


def compose_kernel(
    lt, basis, ct, ni_h, nc_h, li_h, ci_h, cc_h, mi_h, mcount_h, ti_h,
    wide, nidx, rel, crel, meta,
    ni, nc, li, ci, cc, mi, mcount, ti, lts, cts, turned, flat, sems,
):
    copies = fetch(
        sems, (ni_h, ni), (nc_h, nc), (li_h, li), (ci_h, ci), (cc_h, cc), (mi_h, mi), (mcount_h, mcount), (ti_h, ti)
    )
    device = lax.axis_index("rows")
    lts[...] = lt[...].reshape(1024, 128).astype(F32)
    eye = (iota((128, 128), 0) == iota((128, 128), 1)).astype(BF)
    group = iota((128, 128), 1) // 32
    for m in range(8):
        x = [lts[pl.ds(m * 4 + n, 32, stride=32), :].astype(BF) for n in range(4)]
        x = mm_nt(eye, jnp.concatenate(x, axis=0))
        for n in range(4):
            turned[pl.ds(m * 4 + n, 128, stride=32), :] = jnp.where(group == n, x, 0.0)
    low = iota((32, 128), 1) < 64
    for c in range(64):
        here = slice(c * 128, (c + 1) * 128)
        x = turned[c * 64 : (c + 1) * 64, :].astype(BF)
        r = mm(x, jnp.concatenate([basis[:, here]] * 4, axis=0))
        flat[:, here] = jnp.where(low, r[0:32], r[32:64]).astype(BF)
    cts[:, 0:32] = ct[...].astype(F32)
    for k in range(16):
        w = cts[pl.ds(k, 32, stride=16), :][:, 0:32].T.astype(BF)
        here = slice(k * 512, (k + 1) * 512)
        wide[:, here] = mm(w, flat[:, here]).astype(BF)
    for copy in copies:
        copy.wait()
    slot = iota((6, 128), 0)
    nidx[...] = jnp.where(slot < nc[...].reshape(1, 128), ni[...] - device * 128 + 4, 136)
    rel[...] = li[...] - device * 128
    x = jnp.where(iota((3, 16), 0) < cc[...].reshape(1, 16), ci[...] - device * 16, -100)
    x = jnp.concatenate([x.astype(F32), jnp.zeros((5, 16), F32)], axis=0).T
    crel[...] = jnp.concatenate([x] * 8, axis=0).astype(I32)
    t = jnp.where(iota((8, 64), 1) == device // 4, ti[...], 0)
    meta[0:8, :] = jnp.broadcast_to(jnp.sum(t, axis=1, keepdims=True), (8, 128))
    for j in range(2):
        for s in range(8):
            m = mi[j, s]
            d = m >> 1
            at = (d >> 6) * 64 + (d & 7) * 8 + ((d >> 3) & 7)
            side = jnp.where(s < mcount[j], m & 1, -1)
            meta[8 + j * 8 + s : 9 + j * 8 + s, :] = jnp.where(iota((1, 128), 1) == 0, at, side)


def field_kernel(
    nidx, rel, crel, lc, cl, near_got, far_got, mt,
    vec_h, nb_h, coup_h, ccoup_h, lt_h, basis_h, tc_h, mc_h,
    total, wide, down,
    ml, mr, vec, nb, coup, ccoup, lt, basis, tc, mc, picked, lts, fx, rows, tiles, sems,
):
    copies = fetch(
        sems, (ccoup_h, ccoup), (lt_h, lt), (vec_h, vec), (basis_h, basis),
        *[(coup_h.at[s], coup.at[s]) for s in range(8)],
    )
    later = [
        pltpu.make_async_copy(a, b, sems.at[12 + n])
        for n, (a, b) in enumerate(
            [(nb_h.at[:, :, pl.ds(n * 1024, 1024)], nb.at[n]) for n in range(8)]
            + [(tc_h, tc), (mc_h, mc)]
        )
    ]
    even = lax.axis_index("rows") % 2 == 0
    a, b = near_got[...].astype(F32), far_got[...].astype(F32)
    ml[...] = jnp.where(even, b, a).astype(BF)
    mr[...] = jnp.where(even, a, b).astype(BF)

    lcv = lc[...]
    stack = jnp.concatenate([lcv[:, v * 128 : (v + 1) * 128] for v in range(8)], axis=0)
    mine = iota((256, 128), 0) // 32 == iota((256, 128), 1) // 16
    cols = [stack]
    for ref in (ml, mr):
        edge = jnp.concatenate([ref[0:32, :].astype(F32)] * 8, axis=0)
        cols.append(jnp.where(mine, edge, 0.0).astype(BF))
    lhs = jnp.concatenate(cols, axis=1)
    where = iota((128, 128), 0)
    for s in range(8):
        at = rel[s : s + 1, :]
        onehot = jnp.concatenate(
            [
                (where == at).astype(F32),
                (where % 16 == at + 16).astype(F32),
                (where % 16 == at - 128).astype(F32),
            ],
            axis=0,
        ).astype(BF)
        picked[s] = mm(lhs, onehot)

    for copy in later[:2]:
        copy.start()

    clhs = jnp.concatenate([cl[...], ml[32:64, :], mr[32:64, :]], axis=1)
    row, lane = iota((128, 128), 0), iota((128, 128), 1)
    same = row // 16 == lane // 16
    spread = (iota((32, 512), 0) == iota((32, 512), 1) // 16).astype(BF)
    own = iota((128, 512), 0) % 16 == iota((128, 512), 1) % 16
    copies[0].wait()
    cnear = jnp.zeros((128, 32), F32)
    for s in range(3):
        at = jnp.broadcast_to(crel[:, s : s + 1], (128, 128))
        onehot = jnp.concatenate(
            [
                (same & (lane % 16 == at)).astype(F32),
                (same & (lane % 16 == at + 16)).astype(F32),
                (same & (lane % 16 == at - 16)).astype(F32),
            ],
            axis=1,
        ).astype(BF)
        x = mm_nt(onehot, clhs).astype(BF)
        x = jnp.where(own, mm(x, spread), 0.0).astype(BF)
        cnear = cnear + mm(x, ccoup[s].reshape(512, 32))
    grow = (
        (iota((128, 1024), 0) // 16 == iota((128, 1024), 1) // 128)
        & (iota((128, 1024), 0) % 16 == iota((128, 1024), 1) % 128 // 8)
    ).astype(BF)
    r = mm(cnear.T.astype(BF), grow)
    for v in range(8):
        fx[v * 32 : (v + 1) * 32, :] = r[:, v * 128 : (v + 1) * 128]

    for copy in later[2:]:
        copy.start()
    copies[1].wait()
    lts[...] = lt[...].reshape(1024, 128).astype(F32)

    def down_step(t, sums):
        q0 = t * 4
        for n in range(4):
            w = lts[pl.ds(q0 + n, 32, stride=32), :]
            sums = tuple(
                sums[v] + w * fx[pl.ds(v * 32 + q0 + n, 1), :] for v in range(8)
            )
        return sums

    sums = tuple(jnp.zeros((32, 128), F32) for _ in range(8))
    sums = lax.fori_loop(0, 8, down_step, sums)

    low = iota((8, 128), 1) < 64

    def put(x, at):
        y = pltpu.roll(x, 64, 1)
        tiles[at] = jnp.where(low, x, y)
        tiles[at + 1] = jnp.where(low, y, x)

    copies[2].wait()
    for p in range(64):
        put(vec[:, p * 128 : (p + 1) * 128].astype(F32), 4 + 2 * p)
    for ref, at in ((ml, 0), (mr, 132)):
        pts = ref[64:80, :].astype(F32)
        put(pts[0:8], at)
        put(pts[8:16], at + 2)
    tiles[136] = jnp.zeros((8, 128), F32)

    for t in range(32):
        s, p0 = t // 4, t % 4 * 8
        if t % 4 == 0:
            copies[4 + s].wait()
            later[s].wait()
        for p in range(p0, p0 + 8):
            w = coup[s, p].astype(F32)
            sums = [sums[v] + w * picked[s, v * 32 + p : v * 32 + p + 1, :] for v in range(8)]
        parts = []
        for l in range(4):
            i = t * 4 + l
            parts.append(
                jnp.concatenate(
                    [
                        jnp.where(low, tiles[nidx[2 * n, i]], tiles[nidx[2 * n + 1, i]])
                        for n in range(3)
                    ],
                    axis=1,
                )
            )
        x = jnp.concatenate(parts, axis=0).astype(BF)
        a, c = t * 256, t % 4 * 256
        r = mm(x, nb[t // 4, :, :, c : c + 256].reshape(384, 256))
        total[:, a : a + 128] = jnp.where(low, r[0:8, 0:128], r[8:16, 0:128])
        total[:, a + 128 : a + 256] = jnp.where(low, r[16:24, 128:256], r[24:32, 128:256])

    eye = (iota((128, 128), 0) == iota((128, 128), 1)).astype(BF)
    for v in range(8):
        rows[pl.ds(v, 128, stride=8), 0:32] = mm_nt(eye, sums[v].astype(BF))
    copies[3].wait()
    for c in range(64):
        here = slice(c * 128, (c + 1) * 128)
        r = mm(rows[c * 16 : (c + 1) * 16, 0:32].astype(BF), basis[:, here])
        total[:, here] = total[:, here] + jnp.where(low, r[0:8], r[8:16])

    device = lax.axis_index("rows")
    pick = (iota((8, 64), 1) == device // 4).astype(BF)
    keep = iota((32, 1024), 0) == iota((32, 1024), 1) // 32
    fold = (iota((1024, 32), 0) % 32 == iota((1024, 32), 1)).astype(BF)
    later[8].wait()
    later[9].wait()
    none = jnp.zeros((32, 32), F32)
    for s in range(8):
        x = mm_nt(pick, tc[s].reshape(1024, 64))
        x = jnp.where(keep, jnp.broadcast_to(x[0:1], (32, 1024)), 0.0).astype(BF)
        top = jnp.concatenate([none, none, mm(x, fold), none], axis=1).astype(BF)
        x = mc[s].astype(F32)
        middle = jnp.concatenate([x[:, 0, :], x[:, 1, :], none, none], axis=1).astype(BF)
        for n, x in enumerate((middle, middle, top, top)):
            wide[s * 128 + n * 32 : s * 128 + n * 32 + 32, :] = x
    mtf = mt[...].astype(F32)
    for j in range(2):
        down[j] = mtf[:, j, :].T.astype(BF)


def spread_kernel(got, meta, near_got, far_got, out):
    x = got[...]
    for n in range(32):
        out[n] = x


def tail_kernel(meta, got, wm, down, total, wide, out):
    lane = iota((8, 128), 1) // 32

    def block(d):
        return got[(d >> 6) * 64 + (d & 7) * 8 + ((d >> 3) & 7)].astype(F32)

    rows = [[], [], []]
    for s in range(8):
        for j in range(2):
            x = got[meta[8 + j * 8 + s, 0]].astype(F32)
            rows[j].append(jnp.where(lane == meta[8 + j * 8 + s, 1], x, 0.0))
        t = meta[s, 0]
        x = (block(4 * t) + block(4 * t + 1)) + (block(4 * t + 2) + block(4 * t + 3))
        rows[2].append(jnp.where(lane >= 2, x, 0.0))
    x = jnp.concatenate([jnp.concatenate(r, axis=1) for r in rows], axis=0).astype(BF)
    x = mm(x, wm[...])
    field = x[16:24, 64:96].astype(BF)
    for j in range(2):
        f = x[j * 8 : (j + 1) * 8, j * 32 : (j + 1) * 32] + mm(field, down[j])
        f = f.astype(BF)
        here = slice(j * 4096, (j + 1) * 4096)
        out[:, here] = (total[:, here] + mm(f, wide[:, here])).astype(BF)


def vm():
    return pl.BlockSpec(memory_space=pltpu.VMEM)


def sm():
    return pl.BlockSpec(memory_space=pltpu.SMEM)


def hbm():
    return pl.BlockSpec(memory_space=pltpu.HBM)


def far_away(x):
    return pltpu.with_memory_space_constraint(x, pltpu.HBM)


def params(mib):
    return pltpu.CompilerParams(vmem_limit_bytes=mib * MIB)


def cost(flops, nbytes):
    return pl.CostEstimate(flops=flops, bytes_accessed=nbytes, transcendentals=0)


def body(
    vectors,
    basis_leaf,
    near_block,
    near_index,
    near_count,
    leaf_trans,
    leaf_coupling,
    leaf_index,
    cluster_trans,
    cluster_coupling,
    cluster_index,
    cluster_count,
    middle_trans,
    middle_coupling,
    middle_index,
    middle_count,
    top_coupling,
    top_index,
):
    S = jax.ShapeDtypeStruct
    V = pltpu.VMEM
    DMA = pltpu.SemaphoreType.DMA
    ct_rows = jnp.transpose(cluster_trans, (0, 2, 1)).reshape(512, 32)
    mt_rows = jnp.transpose(middle_trans, (0, 2, 1))
    payload, near_msg, far_msg, lc, cl, basis, lt, ct, mt = pl.pallas_call(
        upward_kernel,
        out_shape=(
            S((8, 8, 128), BF), S((80, 128), BF), S((80, 128), BF), S((32, 1024), BF), S((32, 128), BF),
            S((32, 8192), BF), S((32, 32, 128), BF), S((512, 32), BF), S((32, 2, 32), BF),
        ),
        in_specs=[hbm()] * 5,
        out_specs=(vm(),) * 9,
        scratch_shapes=[V((8, 8192), BF), V((1024, 128), F32), V((32, 1024), F32), DMA((5,))],
        compiler_params=params(16),
        cost_estimate=cost(10**8, 1 * MIB),
        name="upward",
    )(*map(far_away, (vectors, basis_leaf, leaf_trans, ct_rows, mt_rows)))

    def device_id(x, z, y, c):
        return ((x * 8 + z) * 4 + y) * 2 + c

    rest = [(x, y, c) for x in range(4) for y in range(4) for c in range(2)]
    along_z = [[device_id(x, z, y, c) for z in range(8)] for x, y, c in rest]
    across = [[device_id(x, z, y, c) for x, y, c in rest] for z in range(8)]
    got = lax.all_to_all(payload, "rows", 0, 0, axis_index_groups=along_z, tiled=True)

    far_got = lax.ppermute(
        far_msg, "rows", [(i, ((i + 1) ^ 1) - 1) for i in range(1, 255)]
    )
    near_got = lax.ppermute(near_msg, "rows", [(i, i ^ 1) for i in range(256)])

    bases, nidx, rel, crel, meta = pl.pallas_call(
        compose_kernel,
        out_shape=(
            S((32, 8192), BF), S((6, 128), I32), S((8, 128), I32), S((128, 8), I32), S((24, 128), I32),
        ),
        in_specs=[vm()] * 3 + [hbm()] * 8,
        out_specs=(vm(),) * 5,
        scratch_shapes=[
            V((6, 128), I32), V((128,), I32), V((8, 128), I32), V((3, 16), I32), V((16,), I32),
            pltpu.SMEM((2, 8), I32), pltpu.SMEM((2,), I32), V((8, 64), I32),
            V((1024, 128), F32), V((512, 128), F32), V((4096, 128), F32), V((32, 8192), BF),
            DMA((8,)),
        ],
        compiler_params=params(16),
        cost_estimate=cost(10**9, 2 * MIB),
        name="compose",
    )(
        lt, basis, ct,
        *map(
            far_away,
            (
                near_index, near_count, leaf_index, cluster_index, cluster_count,
                jnp.transpose(middle_index), middle_count, top_index,
            ),
        ),
    )

    got = pl.pallas_call(
        spread_kernel,
        out_shape=S((32, 64, 128), BF),
        in_specs=[vm()] * 4,
        out_specs=vm(),
        compiler_params=params(16),
        cost_estimate=cost(10**5, MIB // 2),
        name="spread",
    )(got.reshape(64, 128), meta, near_got, far_got)
    got = lax.all_to_all(got, "rows", 0, 0, axis_index_groups=across, tiled=True)
    got = got.reshape(256, 8, 128)

    total, tables, down = pl.pallas_call(
        field_kernel,
        out_shape=(S((8, 8192), F32), S((1024, 128), BF), S((2, 32, 32), BF)),
        in_specs=[sm()] + [vm()] * 7 + [hbm()] * 8,
        out_specs=(vm(),) * 3,
        scratch_shapes=[
            V((80, 128), BF), V((80, 128), BF), V((8, 8192), BF), V((8, 6, 64, 1024), BF),
            V((8, 32, 32, 128), BF), V((3, 32, 16, 32), BF), V((32, 32, 128), BF), V((32, 8192), BF),
            V((8, 32, 32, 64), BF), V((8, 32, 2, 32), BF),
            V((8, 256, 128), F32), V((1024, 128), F32), V((256, 128), F32), V((1024, 128), F32),
            V((137, 8, 128), F32), DMA((22,)),
        ],
        compiler_params=params(32),
        cost_estimate=cost(2 * 10**9, 12 * MIB),
        name="field",
    )(
        nidx, rel, crel, lc, cl, near_got, far_got, mt,
        *map(
            far_away,
            (
                vectors, near_block, leaf_coupling, jnp.transpose(cluster_coupling, (0, 1, 3, 2)),
                leaf_trans, basis_leaf, top_coupling, jnp.transpose(middle_coupling, (0, 1, 3, 2)),
            ),
        ),
    )

    return pl.pallas_call(
        tail_kernel,
        out_shape=S((8, 8192), BF),
        in_specs=[sm()] + [vm()] * 5,
        out_specs=vm(),
        compiler_params=params(16),
        cost_estimate=cost(10**8, 2 * MIB),
        name="tail",
    )(meta, got, tables, down, total, bases)


def solution(mesh):
    in_specs = (
        P(None, "rows"),
        P(None, "rows"),
        P(None, None, "rows"),
        P(None, "rows"),
        P("rows"),
        P(None, None, "rows"),
        P(None, None, None, "rows"),
        P(None, "rows"),
        P(None, None, "rows"),
        P(None, None, None, "rows"),
        P(None, "rows"),
        P("rows"),
        P(None, None, "rows"),
        P(None, None, None, "rows"),
        P(None, "rows"),
        P("rows"),
        P(),
        P(),
    )
    out_specs = P(None, "rows")
    return jax.shard_map(body, mesh=mesh, in_specs=in_specs, out_specs=out_specs, check_vma=False)
```

```python
import jax
import jax.numpy as jnp
from jax import lax
from jax.experimental import pallas as pl
from jax.experimental.pallas import tpu as pltpu
from jax.sharding import PartitionSpec as P

F32 = jnp.float32
BF = jnp.bfloat16
I32 = jnp.int32
NT = (((1,), (1,)), ((), ()))
MIB = 1 << 20


def iota(shape, dim):
    return lax.broadcasted_iota(I32, shape, dim)


def mm(a, b):
    return jnp.dot(a, b, preferred_element_type=F32)


def mm_nt(a, b):
    return lax.dot_general(a, b, NT, preferred_element_type=F32)


def halves(x):
    hi = x.astype(BF)
    return hi, (x - hi.astype(F32)).astype(BF)


def fetch(sems, *pairs):
    copies = [pltpu.make_async_copy(a, b, sems.at[n]) for n, (a, b) in enumerate(pairs)]
    for c in copies:
        c.start()
    return copies


def upward_kernel(
    vec_h, basis_h, lt_h, ct_h, mt_h,
    payload, near_msg, far_msg, lc, cl, basis, lt, ct, mt,
    vec, rows, lcs, sems,
):
    copies = fetch(sems, (vec_h, vec), (basis_h, basis), (mt_h, mt), (lt_h, lt), (ct_h, ct))
    even = lax.axis_index("rows") % 2 == 0
    own = (iota((32, 256), 1) // 64 == iota((32, 256), 0) // 8).astype(F32)
    eye = (iota((32, 32), 0) == iota((32, 32), 1)).astype(BF)
    for copy in copies[:3]:
        copy.wait()
    mtf = mt[...].astype(F32)
    mtj = [mtf[:, j, :].astype(BF) for j in range(2)]
    for c in range(32):
        x = vec[:, c * 256 : (c + 1) * 256].astype(F32)
        x = (jnp.concatenate([x] * 4, axis=0) * own).astype(BF)
        rows[c * 32 : (c + 1) * 32, 0:32] = mm_nt(x, basis[:, c * 256 : (c + 1) * 256])
    group = iota((32, 128), 1) // 16
    first = jnp.zeros((32, 128), F32)
    last = jnp.zeros((32, 128), F32)
    for v in range(8):
        x = rows[pl.ds(v, 128, stride=8), :][:, 0:32].astype(BF)
        x = mm_nt(eye, x)
        lcs[:, v * 128 : (v + 1) * 128] = x
        first = jnp.where(group == v, pltpu.roll(x, v * 16, 1) if v else x, first)
        last = jnp.where(group == v, pltpu.roll(x, v * 16 + 16, 1) if v < 7 else x, last)
    lc[...] = lcs[...].astype(BF)
    copies[3].wait()
    sums = [jnp.zeros((32, 128), F32) for _ in range(8)]
    for r in range(32):
        w = lt[r].astype(F32)
        for v in range(8):
            sums[v] = sums[v] + w * lcs[r : r + 1, v * 128 : (v + 1) * 128]
    hi, lo = halves(jnp.concatenate(sums, axis=0))
    spread = (iota((128, 128), 0) // 8 == iota((128, 128), 1) % 16).astype(BF)
    y = mm(hi, spread) + mm(lo, spread)
    c = jnp.zeros((32, 128), F32)
    for v in range(8):
        c = jnp.where(group == v, y[v * 32 : (v + 1) * 32], c)
    y = jnp.concatenate([y] * 4, axis=1)
    y = jnp.where(iota((256, 512), 0) % 32 == iota((256, 512), 1) // 16, y, 0.0).astype(BF)
    gather = (iota((8, 256), 0) == iota((8, 256), 1) // 32).astype(BF)
    y = mm(gather, y)
    half = iota((8, 512), 1) % 16 // 8
    copies[4].wait()
    pieces = []
    top = jnp.zeros((8, 32), F32)
    for j in range(2):
        m = mm(jnp.where(half == j, y, 0.0).astype(BF), ct[...]).astype(BF)
        pieces.append(m.astype(F32))
        top = top + mm(m, mtj[j])
    hi = top.astype(BF).astype(F32)
    out = jnp.concatenate(pieces + [hi, top - hi], axis=1).astype(BF)
    for z in range(16):
        payload[z] = out
    c = c.astype(BF)
    cl[...] = c
    head = vec[:, 0:256].astype(F32)
    tail = vec[:, 8192 - 256 : 8192].astype(F32)
    for ref, right in ((near_msg, even), (far_msg, jnp.logical_not(even))):
        ref[0:32, :] = jnp.where(right, last, first).astype(BF)
        ref[32:64, :] = c
        pts = jnp.where(right, tail, head)
        ref[64:80, :] = jnp.concatenate([pts[:, 0:128], pts[:, 128:256]], axis=0).astype(BF)


def compose_kernel(
    lt, basis, ct, ni_h, nc_h, li_h, ci_h, cc_h, mi_h, mcount_h, ti_h,
    wide, flat, nidx, rel, crel, meta,
    ni, nc, li, ci, cc, mi, mcount, ti, lts, cts, turned, sems,
):
    copies = fetch(
        sems, (ni_h, ni), (nc_h, nc), (li_h, li), (ci_h, ci), (cc_h, cc), (mi_h, mi), (mcount_h, mcount), (ti_h, ti)
    )
    device = lax.axis_index("rows")
    lts[...] = lt[...].reshape(1024, 128).astype(F32)
    eye = (iota((128, 128), 0) == iota((128, 128), 1)).astype(BF)
    group = iota((128, 128), 1) // 32
    for m in range(8):
        x = [lts[pl.ds(m * 4 + n, 32, stride=32), :].astype(BF) for n in range(4)]
        x = mm_nt(eye, jnp.concatenate(x, axis=0))
        for n in range(4):
            turned[pl.ds(m * 4 + n, 128, stride=32), :] = jnp.where(group == n, x, 0.0)
    low = iota((32, 128), 1) < 64
    for c in range(64):
        here = slice(c * 128, (c + 1) * 128)
        x = turned[c * 64 : (c + 1) * 64, :].astype(BF)
        r = mm(x, jnp.concatenate([basis[:, here]] * 4, axis=0))
        flat[:, here] = jnp.where(low, r[0:32], r[32:64]).astype(BF)
    cts[:, 0:32] = ct[...].astype(F32)
    for k in range(16):
        w = cts[pl.ds(k, 32, stride=16), :][:, 0:32].T.astype(BF)
        here = slice(k * 512, (k + 1) * 512)
        wide[:, here] = mm(w, flat[:, here]).astype(BF)
    for copy in copies:
        copy.wait()
    slot = iota((6, 128), 0)
    nidx[...] = jnp.where(slot < nc[...].reshape(1, 128), ni[...] - device * 128 + 4, 136)
    rel[...] = li[...] - device * 128
    x = jnp.where(iota((3, 16), 0) < cc[...].reshape(1, 16), ci[...] - device * 16, -100)
    x = jnp.concatenate([x.astype(F32), jnp.zeros((5, 16), F32)], axis=0).T
    crel[...] = jnp.concatenate([x] * 8, axis=0).astype(I32)
    t = jnp.where(iota((8, 64), 1) == device // 4, ti[...], 0)
    meta[0:8, :] = jnp.broadcast_to(jnp.sum(t, axis=1, keepdims=True), (8, 128))
    for j in range(2):
        for s in range(8):
            m = mi[j, s]
            d = m >> 1
            at = (d >> 6) * 64 + ((d >> 1) & 3) * 16 + ((d >> 3) & 7) * 2 + (d & 1)
            side = jnp.where(s < mcount[j], m & 1, -1)
            meta[8 + j * 8 + s : 9 + j * 8 + s, :] = jnp.where(iota((1, 128), 1) == 0, at, side)


def field_kernel(
    nidx, rel, crel, lc, cl, near_got, far_got, mt, flat,
    vec_h, nb_h, coup_h, ccoup_h, basis_h, tc_h, mc_h,
    total, wide, down,
    ml, mr, vec, nb, coup, ccoup, basis, tc, mc, picked, partial, rows, tiles, sems,
):
    order = [(vec_h, vec), (ccoup_h, ccoup), (mc_h, mc)]
    for s in range(8):
        order.append((coup_h.at[s], coup.at[s]))
        order.append((nb_h.at[:, :, pl.ds(s * 1024, 1024)], nb.at[s]))
        order.append((tc_h.at[s], tc.at[s]))
    order.append((basis_h, basis))
    copies = [pltpu.make_async_copy(a, b, sems.at[n]) for n, (a, b) in enumerate(order)]

    def start(first, last):
        for copy in copies[first:last]:
            copy.start()

    start(0, 9)
    even = lax.axis_index("rows") % 2 == 0
    a, b = near_got[...].astype(F32), far_got[...].astype(F32)
    ml[...] = jnp.where(even, b, a).astype(BF)
    mr[...] = jnp.where(even, a, b).astype(BF)

    lcv = lc[...]
    stack = jnp.concatenate([lcv[:, v * 128 : (v + 1) * 128] for v in range(8)], axis=0)
    lane = iota((32, 128), 1)
    left, right = ml[0:32, :].astype(F32), mr[0:32, :].astype(F32)
    edge = []
    for v in range(8):
        a = pltpu.roll(left, 128 - v * 16, 1) if v else left
        b = pltpu.roll(right, (144 - v * 16) % 128, 1) if v != 1 else right
        edge.append(jnp.where(lane < 16, a, b))
    edge = jnp.concatenate(edge, axis=0)[:, 0:32].astype(BF)
    lhs = jnp.concatenate([stack, edge], axis=1)
    where = iota((160, 128), 0)
    where = where - jnp.where(where < 128, 0, jnp.where(where < 144, 144, 16))
    for s in range(0, 8, 2):
        onehot = [(where == rel[n : n + 1, :]).astype(F32) for n in (s, s + 1)]
        x = mm(lhs, jnp.concatenate(onehot, axis=1).astype(BF))
        picked[s] = x[:, 0:128]
        picked[s + 1] = x[:, 128:256]
    low = iota((8, 128), 1) < 64

    def put(x, at):
        y = pltpu.roll(x, 64, 1)
        tiles[at] = jnp.where(low, x, y)
        tiles[at + 1] = jnp.where(low, y, x)

    copies[0].wait()
    for p in range(64):
        put(vec[:, p * 128 : (p + 1) * 128].astype(F32), 4 + 2 * p)
    for ref, at in ((ml, 0), (mr, 132)):
        pts = ref[64:80, :].astype(F32)
        put(pts[0:8], at)
        put(pts[8:16], at + 2)
    tiles[136] = jnp.zeros((8, 128), F32)

    row, lane = iota((128, 128), 0), iota((128, 128), 1)
    same = row // 16 == lane // 16
    spread = (iota((32, 512), 0) == iota((32, 512), 1) // 16).astype(BF)
    own = iota((128, 512), 0) % 16 == iota((128, 512), 1) % 16
    partners = []

    def cluster_pick():
        clhs = jnp.concatenate([cl[...], ml[32:64, :], mr[32:64, :]], axis=1)
        for s in range(3):
            at = jnp.broadcast_to(crel[:, s : s + 1], (128, 128))
            onehot = [same & (lane % 16 == at + n) for n in (0, 16, -16)]
            onehot = jnp.concatenate([o.astype(F32) for o in onehot], axis=1).astype(BF)
            partners.append(mm_nt(onehot, clhs).astype(BF))

    def cluster_couple():
        copies[1].wait()
        field = jnp.zeros((128, 32), F32)
        for s in range(3):
            x = jnp.where(own, mm(partners[s], spread), 0.0).astype(BF)
            field = field + mm(x, ccoup[s].reshape(512, 32))
        partners.append(field)

    def cluster_store():
        partial[:, 0:32] = partners[3]

    device = lax.axis_index("rows")
    pick = (iota((8, 64), 1) == device // 4).astype(BF)
    keep = iota((32, 1024), 0) == iota((32, 1024), 1) // 32
    fold = (iota((1024, 32), 0) % 32 == iota((1024, 32), 1)).astype(BF)
    none = jnp.zeros((32, 32), F32)

    def top_table(s):
        x = mm_nt(pick, tc[s].reshape(1024, 64))
        x = jnp.where(keep, jnp.broadcast_to(x[0:1], (32, 1024)), 0.0).astype(BF)
        top = jnp.concatenate([none, none, mm(x, fold), none], axis=1).astype(BF)
        wide[s * 128 + 64 : s * 128 + 96, :] = top
        wide[s * 128 + 96 : s * 128 + 128, :] = top

    def middle_table(s):
        x = mc[s].astype(F32)
        middle = jnp.concatenate([x[:, 0, :], x[:, 1, :], none, none], axis=1).astype(BF)
        wide[s * 128 : s * 128 + 32, :] = middle
        wide[s * 128 + 32 : s * 128 + 64, :] = middle

    sums = [jnp.zeros((32, 128), F32) for _ in range(8)]
    for t in range(32):
        s, p0 = t // 4, t % 4 * 8
        if t % 4 == 0:
            for copy in copies[3 + s * 3 : 6 + s * 3]:
                copy.wait()
            if s < 7:
                start(9 + s * 3, min(12 + s * 3, 28))
        for p in range(p0, p0 + 8):
            w = coup[s, p].astype(F32)
            sums = [sums[v] + w * picked[s, v * 32 + p : v * 32 + p + 1, :] for v in range(8)]
        parts = []
        for l in range(4):
            i = t * 4 + l
            parts.append(
                jnp.concatenate(
                    [
                        jnp.where(low, tiles[nidx[2 * n, i]], tiles[nidx[2 * n + 1, i]])
                        for n in range(3)
                    ],
                    axis=1,
                )
            )
        x = jnp.concatenate(parts, axis=0).astype(BF)
        a, c = t * 256, t % 4 * 256
        r = mm(x, nb[s, :, :, c : c + 256].reshape(384, 256))
        total[:, a : a + 128] = jnp.where(low, r[0:8, 0:128], r[8:16, 0:128])
        total[:, a + 128 : a + 256] = jnp.where(low, r[16:24, 128:256], r[24:32, 128:256])
        if t % 4 == 1:
            top_table(s)
        if t == 2:
            cluster_pick()
        if t == 6:
            cluster_couple()
        if t == 10:
            cluster_store()
            copies[2].wait()
        if t >= 11 and t % 2 == 0 and t < 27:
            middle_table((t - 12) // 2)

    mtf = mt[...].astype(F32)
    for j in range(2):
        down[j] = mtf[:, j, :].T.astype(BF)
    eye = (iota((128, 128), 0) == iota((128, 128), 1)).astype(BF)
    for v in range(8):
        rows[pl.ds(v, 128, stride=8), 0:32] = mm_nt(eye, sums[v].astype(BF))
    copies[27].wait()
    for k in range(16):
        x = partial[pl.ds(k, 8, stride=16), :][:, 0:32].astype(BF)
        here = slice(k * 512, (k + 1) * 512)
        total[:, here] = total[:, here] + mm(x, flat[:, here])
    for c in range(64):
        here = slice(c * 128, (c + 1) * 128)
        r = mm(rows[c * 16 : (c + 1) * 16, 0:32].astype(BF), basis[:, here])
        total[:, here] = total[:, here] + jnp.where(low, r[0:8], r[8:16])


def spread_kernel(got, meta, near_got, far_got, out):
    x = got[...]
    for n in range(16):
        out[n] = x


def tail_kernel(meta, got, wm, down, total, wide, out):
    lane = iota((8, 128), 1) // 32

    def block(d):
        return got[(d >> 6) * 64 + ((d >> 1) & 3) * 16 + ((d >> 3) & 7) * 2 + (d & 1)].astype(F32)

    rows = [[], [], []]
    for s in range(8):
        for j in range(2):
            x = got[meta[8 + j * 8 + s, 0]].astype(F32)
            rows[j].append(jnp.where(lane == meta[8 + j * 8 + s, 1], x, 0.0))
        t = meta[s, 0]
        x = (block(4 * t) + block(4 * t + 1)) + (block(4 * t + 2) + block(4 * t + 3))
        rows[2].append(jnp.where(lane >= 2, x, 0.0))
    x = jnp.concatenate([jnp.concatenate(r, axis=1) for r in rows], axis=0).astype(BF)
    x = mm(x, wm[...])
    field = x[16:24, 64:96].astype(BF)
    for j in range(2):
        f = x[j * 8 : (j + 1) * 8, j * 32 : (j + 1) * 32] + mm(field, down[j])
        f = f.astype(BF)
        here = slice(j * 4096, (j + 1) * 4096)
        out[:, here] = (total[:, here] + mm(f, wide[:, here])).astype(BF)


def vm():
    return pl.BlockSpec(memory_space=pltpu.VMEM)


def sm():
    return pl.BlockSpec(memory_space=pltpu.SMEM)


def hbm():
    return pl.BlockSpec(memory_space=pltpu.HBM)


def far_away(x):
    return pltpu.with_memory_space_constraint(x, pltpu.HBM)


def params(mib):
    return pltpu.CompilerParams(vmem_limit_bytes=mib * MIB)


def cost(flops, nbytes):
    return pl.CostEstimate(flops=flops, bytes_accessed=nbytes, transcendentals=0)


def body(
    vectors,
    basis_leaf,
    near_block,
    near_index,
    near_count,
    leaf_trans,
    leaf_coupling,
    leaf_index,
    cluster_trans,
    cluster_coupling,
    cluster_index,
    cluster_count,
    middle_trans,
    middle_coupling,
    middle_index,
    middle_count,
    top_coupling,
    top_index,
):
    S = jax.ShapeDtypeStruct
    V = pltpu.VMEM
    DMA = pltpu.SemaphoreType.DMA
    ct_rows = jnp.transpose(cluster_trans, (0, 2, 1)).reshape(512, 32)
    mt_rows = jnp.transpose(middle_trans, (0, 2, 1))
    payload, near_msg, far_msg, lc, cl, basis, lt, ct, mt = pl.pallas_call(
        upward_kernel,
        out_shape=(
            S((16, 8, 128), BF), S((80, 128), BF), S((80, 128), BF), S((32, 1024), BF), S((32, 128), BF),
            S((32, 8192), BF), S((32, 32, 128), BF), S((512, 32), BF), S((32, 2, 32), BF),
        ),
        in_specs=[hbm()] * 5,
        out_specs=(vm(),) * 9,
        scratch_shapes=[V((8, 8192), BF), V((1024, 128), F32), V((32, 1024), F32), DMA((5,))],
        compiler_params=params(16),
        cost_estimate=cost(10**8, 1 * MIB),
        name="upward",
    )(*map(far_away, (vectors, basis_leaf, leaf_trans, ct_rows, mt_rows)))

    def device_id(x, z, y, c):
        return ((x * 8 + z) * 4 + y) * 2 + c

    flat = [(x, y) for x in range(4) for y in range(4)]
    deep = [(z, c) for z in range(8) for c in range(2)]
    along_z = [[device_id(x, z, y, c) for z, c in deep] for x, y in flat]
    across = [[device_id(x, z, y, c) for x, y in flat] for z, c in deep]
    got = lax.all_to_all(payload, "rows", 0, 0, axis_index_groups=along_z, tiled=True)

    far_got = lax.ppermute(
        far_msg, "rows", [(i, (((i + 1) ^ 1) - 1) % 256) for i in range(256)]
    )
    near_got = lax.ppermute(near_msg, "rows", [(i, i ^ 1) for i in range(256)])

    bases, leaf_bases, nidx, rel, crel, meta = pl.pallas_call(
        compose_kernel,
        out_shape=(
            S((32, 8192), BF), S((32, 8192), BF), S((6, 128), I32), S((8, 128), I32), S((128, 8), I32), S((24, 128), I32),
        ),
        in_specs=[vm()] * 3 + [hbm()] * 8,
        out_specs=(vm(),) * 6,
        scratch_shapes=[
            V((6, 128), I32), V((128,), I32), V((8, 128), I32), V((3, 16), I32), V((16,), I32),
            pltpu.SMEM((2, 8), I32), pltpu.SMEM((2,), I32), V((8, 64), I32),
            V((1024, 128), F32), V((512, 128), F32), V((4096, 128), F32), DMA((8,)),
        ],
        compiler_params=params(16),
        cost_estimate=cost(10**9, 2 * MIB),
        name="compose",
    )(
        lt, basis, ct,
        *map(
            far_away,
            (
                near_index, near_count, leaf_index, cluster_index, cluster_count,
                jnp.transpose(middle_index), middle_count, top_index,
            ),
        ),
    )

    got = pl.pallas_call(
        spread_kernel,
        out_shape=S((16, 128, 128), BF),
        in_specs=[vm()] * 4,
        out_specs=vm(),
        compiler_params=params(16),
        cost_estimate=cost(10**5, MIB // 2),
        name="spread",
    )(got.reshape(128, 128), meta, near_got, far_got)
    got = lax.all_to_all(got, "rows", 0, 0, axis_index_groups=across, tiled=True)
    got = got.reshape(256, 8, 128)

    total, tables, down = pl.pallas_call(
        field_kernel,
        out_shape=(S((8, 8192), F32), S((1024, 128), BF), S((2, 32, 32), BF)),
        in_specs=[sm()] + [vm()] * 8 + [hbm()] * 7,
        out_specs=(vm(),) * 3,
        scratch_shapes=[
            V((80, 128), BF), V((80, 128), BF), V((8, 8192), BF), V((8, 6, 64, 1024), BF),
            V((8, 32, 32, 128), BF), V((3, 32, 16, 32), BF), V((32, 8192), BF),
            V((8, 32, 32, 64), BF), V((8, 32, 2, 32), BF),
            V((8, 256, 128), F32), V((128, 128), F32), V((1024, 128), F32),
            V((137, 8, 128), F32), DMA((28,)),
        ],
        compiler_params=params(32),
        cost_estimate=cost(2 * 10**9, 12 * MIB),
        name="field",
    )(
        nidx, rel, crel, lc, cl, near_got, far_got, mt, leaf_bases,
        *map(
            far_away,
            (
                vectors, near_block, leaf_coupling, jnp.transpose(cluster_coupling, (0, 1, 3, 2)),
                basis_leaf, top_coupling, jnp.transpose(middle_coupling, (0, 1, 3, 2)),
            ),
        ),
    )

    return pl.pallas_call(
        tail_kernel,
        out_shape=S((8, 8192), BF),
        in_specs=[sm()] + [vm()] * 5,
        out_specs=vm(),
        compiler_params=params(16),
        cost_estimate=cost(10**8, 2 * MIB),
        name="tail",
    )(meta, got, tables, down, total, bases)


def solution(mesh):
    in_specs = (
        P(None, "rows"),
        P(None, "rows"),
        P(None, None, "rows"),
        P(None, "rows"),
        P("rows"),
        P(None, None, "rows"),
        P(None, None, None, "rows"),
        P(None, "rows"),
        P(None, None, "rows"),
        P(None, None, None, "rows"),
        P(None, "rows"),
        P("rows"),
        P(None, None, "rows"),
        P(None, None, None, "rows"),
        P(None, "rows"),
        P("rows"),
        P(),
        P(),
    )
    out_specs = P(None, "rows")
    return jax.shard_map(body, mesh=mesh, in_specs=in_specs, out_specs=out_specs, check_vma=False)
```

```python
import jax
import jax.numpy as jnp
from jax import lax
from jax.experimental import pallas as pl
from jax.experimental.pallas import tpu as pltpu
from jax.sharding import PartitionSpec as P

F32 = jnp.float32
BF = jnp.bfloat16
I32 = jnp.int32
NT = (((1,), (1,)), ((), ()))
MIB = 1 << 20


def iota(shape, dim):
    return lax.broadcasted_iota(I32, shape, dim)


def mm(a, b):
    return jnp.dot(a, b, preferred_element_type=F32)


def mm_nt(a, b):
    return lax.dot_general(a, b, NT, preferred_element_type=F32)


def halves(x):
    hi = x.astype(BF)
    return hi, (x - hi.astype(F32)).astype(BF)


def fetch(sems, *pairs):
    copies = [pltpu.make_async_copy(a, b, sems.at[n]) for n, (a, b) in enumerate(pairs)]
    for c in copies:
        c.start()
    return copies


def upward_kernel(
    vec_h, basis_h, lt_h, ct_h, mt_h,
    payload, near_msg, far_msg, lc, cl, basis, lt, ct, mt,
    vec, rows, lcs, sems,
):
    copies = fetch(sems, (vec_h, vec), (basis_h, basis), (mt_h, mt), (lt_h, lt), (ct_h, ct))
    even = lax.axis_index("rows") % 2 == 0
    own = (iota((32, 256), 1) // 64 == iota((32, 256), 0) // 8).astype(F32)
    eye = (iota((32, 32), 0) == iota((32, 32), 1)).astype(BF)
    for copy in copies:
        copy.wait()
    mtf = mt[...].astype(F32)
    mtj = [mtf[:, j, :].astype(BF) for j in range(2)]
    for c in range(32):
        x = vec[:, c * 256 : (c + 1) * 256].astype(F32)
        x = (jnp.concatenate([x] * 4, axis=0) * own).astype(BF)
        rows[c * 32 : (c + 1) * 32, 0:32] = mm_nt(x, basis[:, c * 256 : (c + 1) * 256])
    group = iota((32, 128), 1) // 16
    first = jnp.zeros((32, 128), F32)
    last = jnp.zeros((32, 128), F32)
    for v in range(8):
        x = rows[pl.ds(v, 128, stride=8), :][:, 0:32].astype(BF)
        x = mm_nt(eye, x)
        lcs[:, v * 128 : (v + 1) * 128] = x
        first = jnp.where(group == v, pltpu.roll(x, v * 16, 1) if v else x, first)
        last = jnp.where(group == v, pltpu.roll(x, v * 16 + 16, 1) if v < 7 else x, last)
    lc[...] = lcs[...].astype(BF)
    sums = [jnp.zeros((32, 128), F32) for _ in range(8)]
    for r in range(32):
        w = lt[r].astype(F32)
        for v in range(8):
            sums[v] = sums[v] + w * lcs[r : r + 1, v * 128 : (v + 1) * 128]
    hi, lo = halves(jnp.concatenate(sums, axis=0))
    spread = (iota((128, 128), 0) // 8 == iota((128, 128), 1) % 16).astype(BF)
    y = mm(hi, spread) + mm(lo, spread)
    c = jnp.zeros((32, 128), F32)
    for v in range(8):
        c = jnp.where(group == v, y[v * 32 : (v + 1) * 32], c)
    y = jnp.concatenate([y] * 4, axis=1)
    y = jnp.where(iota((256, 512), 0) % 32 == iota((256, 512), 1) // 16, y, 0.0).astype(BF)
    gather = (iota((8, 256), 0) == iota((8, 256), 1) // 32).astype(BF)
    y = mm(gather, y)
    half = iota((8, 512), 1) % 16 // 8
    pieces = []
    top = jnp.zeros((8, 32), F32)
    for j in range(2):
        m = mm(jnp.where(half == j, y, 0.0).astype(BF), ct[...]).astype(BF)
        pieces.append(m.astype(F32))
        top = top + mm(m, mtj[j])
    hi = top.astype(BF).astype(F32)
    out = jnp.concatenate(pieces + [hi, top - hi], axis=1).astype(BF)
    for z in range(16):
        payload[z] = out
    c = c.astype(BF)
    cl[...] = c
    head = vec[:, 0:256].astype(F32)
    tail = vec[:, 8192 - 256 : 8192].astype(F32)
    for ref, right in ((near_msg, even), (far_msg, jnp.logical_not(even))):
        ref[0:32, :] = jnp.where(right, last, first).astype(BF)
        ref[32:64, :] = c
        pts = jnp.where(right, tail, head)
        ref[64:80, :] = jnp.concatenate([pts[:, 0:128], pts[:, 128:256]], axis=0).astype(BF)


def compose_kernel(
    lt, basis, ct, ni_h, nc_h, li_h, ci_h, cc_h, mi_h, mcount_h, ti_h,
    wide, flat, nidx, rel, crel, meta,
    ni, nc, li, ci, cc, mi, mcount, ti, lts, cts, turned, sems,
):
    copies = fetch(
        sems, (ni_h, ni), (nc_h, nc), (li_h, li), (ci_h, ci), (cc_h, cc), (mi_h, mi), (mcount_h, mcount), (ti_h, ti)
    )
    device = lax.axis_index("rows")
    lts[...] = lt[...].reshape(1024, 128).astype(F32)
    eye = (iota((128, 128), 0) == iota((128, 128), 1)).astype(BF)
    group = iota((128, 128), 1) // 32
    for m in range(8):
        x = [lts[pl.ds(m * 4 + n, 32, stride=32), :].astype(BF) for n in range(4)]
        x = mm_nt(eye, jnp.concatenate(x, axis=0))
        for n in range(4):
            turned[pl.ds(m * 4 + n, 128, stride=32), :] = jnp.where(group == n, x, 0.0)
    low = iota((32, 128), 1) < 64
    for c in range(64):
        here = slice(c * 128, (c + 1) * 128)
        x = turned[c * 64 : (c + 1) * 64, :].astype(BF)
        r = mm(x, jnp.concatenate([basis[:, here]] * 4, axis=0))
        flat[:, here] = jnp.where(low, r[0:32], r[32:64]).astype(BF)
    cts[:, 0:32] = ct[...].astype(F32)
    for k in range(16):
        w = cts[pl.ds(k, 32, stride=16), :][:, 0:32].T.astype(BF)
        here = slice(k * 512, (k + 1) * 512)
        wide[:, here] = mm(w, flat[:, here]).astype(BF)
    for copy in copies:
        copy.wait()
    slot = iota((6, 128), 0)
    nidx[...] = jnp.where(slot < nc[...].reshape(1, 128), ni[...] - device * 128 + 4, 136)
    rel[...] = li[...] - device * 128
    x = jnp.where(iota((3, 16), 0) < cc[...].reshape(1, 16), ci[...] - device * 16, -100)
    x = jnp.concatenate([x.astype(F32), jnp.zeros((5, 16), F32)], axis=0).T
    crel[...] = jnp.concatenate([x] * 8, axis=0).astype(I32)
    t = jnp.where(iota((8, 64), 1) == device // 4, ti[...], 0)
    meta[0:8, :] = jnp.broadcast_to(jnp.sum(t, axis=1, keepdims=True), (8, 128))
    for j in range(2):
        for s in range(8):
            m = mi[j, s]
            d = m >> 1
            at = (d >> 6) * 64 + ((d >> 1) & 3) * 16 + ((d >> 3) & 7) * 2 + (d & 1)
            side = jnp.where(s < mcount[j], m & 1, -1)
            meta[8 + j * 8 + s : 9 + j * 8 + s, :] = jnp.where(iota((1, 128), 1) == 0, at, side)


def field_kernel(
    nidx, rel, crel, lc, cl, near_got, far_got, mt, flat,
    vec_h, nb_h, coup_h, ccoup_h, basis_h, tc_h, mc_h,
    total, wide, down,
    ml, mr, vec, nb, coup, ccoup, basis, tc, mc, picked, partial, rows, tiles, sems,
):
    near_parts = [(nb_h.at[:, :, pl.ds(n * 2048, 2048)], nb.at[n]) for n in range(4)]
    order = [
        (vec_h, vec), (ccoup_h, ccoup), (coup_h, coup), *near_parts[:2],
        (mc_h, mc), (tc_h, tc), *near_parts[2:], (basis_h, basis),
    ]
    copies = fetch(sems, *order)
    even = lax.axis_index("rows") % 2 == 0
    a, b = near_got[...].astype(F32), far_got[...].astype(F32)
    ml[...] = jnp.where(even, b, a).astype(BF)
    mr[...] = jnp.where(even, a, b).astype(BF)

    lcv = lc[...]
    stack = jnp.concatenate([lcv[:, v * 128 : (v + 1) * 128] for v in range(8)], axis=0)
    lane = iota((32, 128), 1)
    left, right = ml[0:32, :].astype(F32), mr[0:32, :].astype(F32)
    edge = []
    for v in range(8):
        a = pltpu.roll(left, 128 - v * 16, 1) if v else left
        b = pltpu.roll(right, (144 - v * 16) % 128, 1) if v != 1 else right
        edge.append(jnp.where(lane < 16, a, b))
    edge = jnp.concatenate(edge, axis=0)[:, 0:32].astype(BF)
    lhs = jnp.concatenate([stack, edge], axis=1)
    where = iota((160, 128), 0)
    where = where - jnp.where(where < 128, 0, jnp.where(where < 144, 144, 16))
    for s in range(0, 8, 2):
        onehot = [(where == rel[n : n + 1, :]).astype(F32) for n in (s, s + 1)]
        x = mm(lhs, jnp.concatenate(onehot, axis=1).astype(BF))
        picked[s] = x[:, 0:128]
        picked[s + 1] = x[:, 128:256]
    low = iota((8, 128), 1) < 64

    def put(x, at):
        y = pltpu.roll(x, 64, 1)
        tiles[at] = jnp.where(low, x, y)
        tiles[at + 1] = jnp.where(low, y, x)

    for copy in copies[0:3]:
        copy.wait()
    for p in range(64):
        put(vec[:, p * 128 : (p + 1) * 128].astype(F32), 4 + 2 * p)
    for ref, at in ((ml, 0), (mr, 132)):
        pts = ref[64:80, :].astype(F32)
        put(pts[0:8], at)
        put(pts[8:16], at + 2)
    tiles[136] = jnp.zeros((8, 128), F32)

    row, lane = iota((128, 128), 0), iota((128, 128), 1)
    same = row // 16 == lane // 16
    spread = (iota((32, 512), 0) == iota((32, 512), 1) // 16).astype(BF)
    own = iota((128, 512), 0) % 16 == iota((128, 512), 1) % 16
    partners = []

    def cluster_pick():
        clhs = jnp.concatenate([cl[...], ml[32:64, :], mr[32:64, :]], axis=1)
        for s in range(3):
            at = jnp.broadcast_to(crel[:, s : s + 1], (128, 128))
            onehot = [same & (lane % 16 == at + n) for n in (0, 16, -16)]
            onehot = jnp.concatenate([o.astype(F32) for o in onehot], axis=1).astype(BF)
            partners.append(mm_nt(onehot, clhs).astype(BF))

    def cluster_couple():
        field = jnp.zeros((128, 32), F32)
        for s in range(3):
            x = jnp.where(own, mm(partners[s], spread), 0.0).astype(BF)
            field = field + mm(x, ccoup[s].reshape(512, 32))
        partners.append(field)

    def cluster_store():
        partial[:, 0:32] = partners[3]

    device = lax.axis_index("rows")
    pick = (iota((8, 64), 1) == device // 4).astype(BF)
    keep = iota((32, 1024), 0) == iota((32, 1024), 1) // 32
    fold = (iota((1024, 32), 0) % 32 == iota((1024, 32), 1)).astype(BF)
    none = jnp.zeros((32, 32), F32)

    def top_table(s):
        x = mm_nt(pick, tc[s].reshape(1024, 64))
        x = jnp.where(keep, jnp.broadcast_to(x[0:1], (32, 1024)), 0.0).astype(BF)
        top = jnp.concatenate([none, none, mm(x, fold), none], axis=1).astype(BF)
        wide[s * 128 + 64 : s * 128 + 96, :] = top
        wide[s * 128 + 96 : s * 128 + 128, :] = top

    def middle_table(s):
        x = mc[s].astype(F32)
        middle = jnp.concatenate([x[:, 0, :], x[:, 1, :], none, none], axis=1).astype(BF)
        wide[s * 128 : s * 128 + 32, :] = middle
        wide[s * 128 + 32 : s * 128 + 64, :] = middle

    def near_part(n):
        parts = []
        for l in range(4):
            i = n * 4 + l
            parts.append(
                jnp.concatenate(
                    [
                        jnp.where(low, tiles[nidx[2 * m, i]], tiles[nidx[2 * m + 1, i]])
                        for m in range(3)
                    ],
                    axis=1,
                )
            )
        x = jnp.concatenate(parts, axis=0).astype(BF)
        a, c = n * 256, n % 8 * 256
        r = mm(x, nb[n // 8, :, :, c : c + 256].reshape(384, 256))
        total[:, a : a + 128] = jnp.where(low, r[0:8, 0:128], r[8:16, 0:128])
        total[:, a + 128 : a + 256] = jnp.where(low, r[16:24, 128:256], r[24:32, 128:256])

    sums = [jnp.zeros((32, 128), F32) for _ in range(8)]
    for t in range(32):
        s, p0 = t // 4, t % 4 * 8
        if t == 16:
            for copy in copies[3:7]:
                copy.wait()
        if t == 24:
            for copy in copies[7:10]:
                copy.wait()
        for p in range(p0, p0 + 8):
            w = coup[s, p].astype(F32)
            sums = [sums[v] + w * picked[s, v * 32 + p : v * 32 + p + 1, :] for v in range(8)]
        for n in (2 * t - 32, 2 * t - 31) if t >= 16 else ():
            near_part(n)
        if t >= 16 and t % 2 == 1:
            top_table((t - 16) // 2)
        if t == 2:
            cluster_pick()
        if t == 6:
            cluster_couple()
        if t == 10:
            cluster_store()
        if t >= 16 and t % 2 == 0:
            middle_table((t - 16) // 2)

    mtf = mt[...].astype(F32)
    for j in range(2):
        down[j] = mtf[:, j, :].T.astype(BF)
    eye = (iota((128, 128), 0) == iota((128, 128), 1)).astype(BF)
    for v in range(8):
        rows[pl.ds(v, 128, stride=8), 0:32] = mm_nt(eye, sums[v].astype(BF))
    for k in range(16):
        x = partial[pl.ds(k, 8, stride=16), :][:, 0:32].astype(BF)
        here = slice(k * 512, (k + 1) * 512)
        total[:, here] = total[:, here] + mm(x, flat[:, here])
    for c in range(64):
        here = slice(c * 128, (c + 1) * 128)
        r = mm(rows[c * 16 : (c + 1) * 16, 0:32].astype(BF), basis[:, here])
        total[:, here] = total[:, here] + jnp.where(low, r[0:8], r[8:16])


def spread_kernel(got, meta, near_got, far_got, out):
    x = got[...]
    for n in range(16):
        out[n] = x


def tail_kernel(meta, got, wm, down, total, wide, out):
    lane = iota((8, 128), 1) // 32

    def block(d):
        return got[(d >> 6) * 64 + ((d >> 1) & 3) * 16 + ((d >> 3) & 7) * 2 + (d & 1)].astype(F32)

    rows = [[], [], []]
    for s in range(8):
        for j in range(2):
            x = got[meta[8 + j * 8 + s, 0]].astype(F32)
            rows[j].append(jnp.where(lane == meta[8 + j * 8 + s, 1], x, 0.0))
        t = meta[s, 0]
        x = (block(4 * t) + block(4 * t + 1)) + (block(4 * t + 2) + block(4 * t + 3))
        rows[2].append(jnp.where(lane >= 2, x, 0.0))
    x = jnp.concatenate([jnp.concatenate(r, axis=1) for r in rows], axis=0).astype(BF)
    x = mm(x, wm[...])
    field = x[16:24, 64:96].astype(BF)
    for j in range(2):
        f = x[j * 8 : (j + 1) * 8, j * 32 : (j + 1) * 32] + mm(field, down[j])
        f = f.astype(BF)
        here = slice(j * 4096, (j + 1) * 4096)
        out[:, here] = (total[:, here] + mm(f, wide[:, here])).astype(BF)


def vm():
    return pl.BlockSpec(memory_space=pltpu.VMEM)


def sm():
    return pl.BlockSpec(memory_space=pltpu.SMEM)


def hbm():
    return pl.BlockSpec(memory_space=pltpu.HBM)


def far_away(x):
    return pltpu.with_memory_space_constraint(x, pltpu.HBM)


def params(mib):
    return pltpu.CompilerParams(vmem_limit_bytes=mib * MIB)


def cost(flops, nbytes):
    return pl.CostEstimate(flops=flops, bytes_accessed=nbytes, transcendentals=0)


def body(
    vectors,
    basis_leaf,
    near_block,
    near_index,
    near_count,
    leaf_trans,
    leaf_coupling,
    leaf_index,
    cluster_trans,
    cluster_coupling,
    cluster_index,
    cluster_count,
    middle_trans,
    middle_coupling,
    middle_index,
    middle_count,
    top_coupling,
    top_index,
):
    S = jax.ShapeDtypeStruct
    V = pltpu.VMEM
    DMA = pltpu.SemaphoreType.DMA
    ct_rows = jnp.transpose(cluster_trans, (0, 2, 1)).reshape(512, 32)
    mt_rows = jnp.transpose(middle_trans, (0, 2, 1))
    payload, near_msg, far_msg, lc, cl, basis, lt, ct, mt = pl.pallas_call(
        upward_kernel,
        out_shape=(
            S((16, 8, 128), BF), S((80, 128), BF), S((80, 128), BF), S((32, 1024), BF), S((32, 128), BF),
            S((32, 8192), BF), S((32, 32, 128), BF), S((512, 32), BF), S((32, 2, 32), BF),
        ),
        in_specs=[hbm()] * 5,
        out_specs=(vm(),) * 9,
        scratch_shapes=[V((8, 8192), BF), V((1024, 128), F32), V((32, 1024), F32), DMA((5,))],
        compiler_params=params(16),
        cost_estimate=cost(10**8, 1 * MIB),
        name="upward",
    )(*map(far_away, (vectors, basis_leaf, leaf_trans, ct_rows, mt_rows)))

    def device_id(x, z, y, c):
        return ((x * 8 + z) * 4 + y) * 2 + c

    flat = [(x, y) for x in range(4) for y in range(4)]
    deep = [(z, c) for z in range(8) for c in range(2)]
    along_z = [[device_id(x, z, y, c) for z, c in deep] for x, y in flat]
    across = [[device_id(x, z, y, c) for x, y in flat] for z, c in deep]
    got = lax.all_to_all(payload, "rows", 0, 0, axis_index_groups=along_z, tiled=True)

    far_got = lax.ppermute(
        far_msg, "rows", [(0, 0), (255, 255)] + [(i, ((i + 1) ^ 1) - 1) for i in range(1, 255)]
    )
    near_got = lax.ppermute(near_msg, "rows", [(i, i ^ 1) for i in range(256)])

    bases, leaf_bases, nidx, rel, crel, meta = pl.pallas_call(
        compose_kernel,
        out_shape=(
            S((32, 8192), BF), S((32, 8192), BF), S((6, 128), I32), S((8, 128), I32), S((128, 8), I32), S((24, 128), I32),
        ),
        in_specs=[vm()] * 3 + [hbm()] * 8,
        out_specs=(vm(),) * 6,
        scratch_shapes=[
            V((6, 128), I32), V((128,), I32), V((8, 128), I32), V((3, 16), I32), V((16,), I32),
            pltpu.SMEM((2, 8), I32), pltpu.SMEM((2,), I32), V((8, 64), I32),
            V((1024, 128), F32), V((512, 128), F32), V((4096, 128), F32), DMA((8,)),
        ],
        compiler_params=params(16),
        cost_estimate=cost(10**9, 2 * MIB),
        name="compose",
    )(
        lt, basis, ct,
        *map(
            far_away,
            (
                near_index, near_count, leaf_index, cluster_index, cluster_count,
                jnp.transpose(middle_index), middle_count, top_index,
            ),
        ),
    )

    got = pl.pallas_call(
        spread_kernel,
        out_shape=S((16, 128, 128), BF),
        in_specs=[vm()] * 4,
        out_specs=vm(),
        compiler_params=params(16),
        cost_estimate=cost(10**5, MIB // 2),
        name="spread",
    )(got.reshape(128, 128), meta, near_got, far_got)
    got = lax.all_to_all(got, "rows", 0, 0, axis_index_groups=across, tiled=True)
    got = got.reshape(256, 8, 128)

    total, tables, down = pl.pallas_call(
        field_kernel,
        out_shape=(S((8, 8192), F32), S((1024, 128), BF), S((2, 32, 32), BF)),
        in_specs=[sm()] + [vm()] * 8 + [hbm()] * 7,
        out_specs=(vm(),) * 3,
        scratch_shapes=[
            V((80, 128), BF), V((80, 128), BF), V((8, 8192), BF), V((4, 6, 64, 2048), BF),
            V((8, 32, 32, 128), BF), V((3, 32, 16, 32), BF), V((32, 8192), BF),
            V((8, 32, 32, 64), BF), V((8, 32, 2, 32), BF),
            V((8, 256, 128), F32), V((128, 128), F32), V((1024, 128), F32),
            V((137, 8, 128), F32), DMA((10,)),
        ],
        compiler_params=params(32),
        cost_estimate=cost(2 * 10**9, 12 * MIB),
        name="field",
    )(
        nidx, rel, crel, lc, cl, near_got, far_got, mt, leaf_bases,
        *map(
            far_away,
            (
                vectors, near_block, leaf_coupling, jnp.transpose(cluster_coupling, (0, 1, 3, 2)),
                basis_leaf, top_coupling, jnp.transpose(middle_coupling, (0, 1, 3, 2)),
            ),
        ),
    )

    return pl.pallas_call(
        tail_kernel,
        out_shape=S((8, 8192), BF),
        in_specs=[sm()] + [vm()] * 5,
        out_specs=vm(),
        compiler_params=params(16),
        cost_estimate=cost(10**8, 2 * MIB),
        name="tail",
    )(meta, got, tables, down, total, bases)


def solution(mesh):
    in_specs = (
        P(None, "rows"),
        P(None, "rows"),
        P(None, None, "rows"),
        P(None, "rows"),
        P("rows"),
        P(None, None, "rows"),
        P(None, None, None, "rows"),
        P(None, "rows"),
        P(None, None, "rows"),
        P(None, None, None, "rows"),
        P(None, "rows"),
        P("rows"),
        P(None, None, "rows"),
        P(None, None, None, "rows"),
        P(None, "rows"),
        P("rows"),
        P(),
        P(),
    )
    out_specs = P(None, "rows")
    return jax.shard_map(body, mesh=mesh, in_specs=in_specs, out_specs=out_specs, check_vma=False)
```
